32 devices in a mesh: tm: 16 (over z, x, core), row: 2 (over y).
Axes of the slice: x: 2, y: 2, z: 4, core: 2. Of those that a mesh axis runs over, the one named last changes fastest.
Arguments:
- slice_ops: bfloat16 [16, 2048, 2048], P('tm', 'row'), may hold values from -6 to 6
- base_op: bfloat16 [2048, 2048], replicated, may hold values from -6 to 6
- load_table: float32 [16, 2048], replicated, may hold values from -1 to 1
- phase_idx: int32 [16, 2], P('tm'), may hold values from 0 to 15
- step_counts: int32 [16, 2], P('tm'), may hold values from 1 to 8
Outputs:
- windows: bfloat16 [16, 2048, 2048], P('tm', 'row')
The draws below stay inside these ranges and needn't reach their ends.
All inputs are finite; a program needn't handle non-finite values.
Results may differ from the reference program's by a relative error of at most 0.012.
Values may be sent and summed in bfloat16 or wider, within the bound.
A program may use at most 128 MiB of HBM per device.

```python
import math
import jax
import jax.numpy as jnp
from jax import lax

S = 2048
PHASES = 16
SUB = 2
LEVELS = 2
SLICES = 16


def plant(result, key, least, top_value):
    shape = result.shape
    index_at = [jax.random.randint(jax.random.fold_in(key, axis), (), 0, shape[axis]) for axis in range(len(shape))]
    result = result.at[tuple(index_at)].set(least)
    longest = shape.index(max(shape))
    index_at[longest] = (index_at[longest] + 1) % shape[longest]
    return result.at[tuple(index_at)].set(top_value)


def level_of(stream_key, extent, pieces, low, top_value):
    loudness = 1.0
    for dim, shards_of in pieces:
        draws = jax.random.uniform(jax.random.fold_in(jax.random.fold_in(stream_key, 6), dim), (shards_of,), jnp.float32, low / len(pieces), top_value / len(pieces))
        loudness = loudness * jnp.repeat(jnp.exp(draws), extent[dim] // shards_of).reshape((-1,) + (1,) * (len(extent) - 1 - dim))
    return loudness


def centred(own_key, dims, scale, bound, pieces=(), kind=jnp.bfloat16):
    loudness = level_of(own_key, dims, pieces, -0.22, 0.18) if pieces else 1.0
    drawn = jax.random.normal(own_key, dims, jnp.float32) * scale * loudness
    return jnp.minimum(jnp.maximum(drawn, -bound), bound).astype(kind)


def setup_inputs(seed: int = 0) -> dict:
    splits = jax.random.split(jax.random.key(seed), 6)
    slice_ops = centred(splits[0], (SLICES, S, S), 1.0, 6.0, ((0, 16), (1, 2)))
    base_op = centred(splits[1], (S, S), 1.0, 6.0)
    load_table = jnp.clip(jax.random.uniform(splits[2], (PHASES, S), jnp.float32, -1.0, 1.0), -1.0, 1.0)
    phase_idx = plant(jax.random.randint(splits[3], (SLICES, SUB), 0, PHASES), jax.random.fold_in(splits[3], 1), 0, PHASES - 1).astype(jnp.int32)
    step_counts = plant(jax.random.randint(splits[4], (SLICES, SUB), 1, 9), jax.random.fold_in(splits[4], 1), 1, 8).astype(jnp.int32)
    return {"slice_ops": slice_ops, "base_op": base_op, "load_table": load_table, "phase_idx": phase_idx, "step_counts": step_counts}


def reference(slice_ops, base_op, load_table, phase_idx, step_counts):
    norm_scale = 1.0 / math.sqrt(S)

    def slice_transfer(operands):
        slice_op, index_row, count_row = operands
        gain_rows = jnp.exp(0.1 * count_row.astype(jnp.float32)[:, None] * load_table[index_row])
        right_factor = (base_op * gain_rows[0]).astype(jnp.bfloat16)
        left_factor = (slice_op * gain_rows[1]).astype(jnp.bfloat16)
        product = jnp.dot(left_factor, right_factor, preferred_element_type=jnp.float32)
        return (product * norm_scale).astype(jnp.bfloat16)
    current = lax.map(slice_transfer, (slice_ops, phase_idx, step_counts))

    def combine_pair(operands):
        later, earlier = operands
        product = jnp.dot(later, earlier, preferred_element_type=jnp.float32)
        return (product * norm_scale).astype(jnp.bfloat16)
    for depth_level in range(LEVELS):
        distance = 2 ** depth_level
        earlier_all = jnp.roll(current, distance, axis=0)
        current = lax.map(combine_pair, (current, earlier_all))
    return current
```

```python
import functools
import math

import jax
import jax.numpy as jnp
from jax import lax
from jax.experimental import pallas as pl
from jax.experimental.pallas import tpu as pltpu
from jax.sharding import PartitionSpec as P

MESH = pl.DeviceIdType.MESH
WIDTH = 256
TILE = 512
LAG = 2


def kernel(
    count, s_hbm, b_hbm, table, phase, steps, o_hbm,
    s, b, p, x, m1, m2, o, s_sem, b_sem, o_sem, send, r1o, r1c, r2o, r2c,
):
    rows, size = s.shape
    chunks = size // WIDTH
    norm = 1.0 / math.sqrt(size)
    k = lax.axis_index("tm")
    r = lax.axis_index("row")
    odd = lax.rem(k, 2)
    even = odd == 0
    own = pl.ds(pl.multiple_of(r * rows, rows), rows)
    cross = pl.ds(pl.multiple_of((1 - r) * rows, rows), rows)

    def cols(n):
        return pl.ds(pl.multiple_of(n * WIDTH, WIDTH), WIDTH)

    def load_b(n):
        return pltpu.make_async_copy(b_hbm.at[:, cols(n)], b.at[:, cols(n)], b_sem.at[n])

    def store_o(n):
        return pltpu.make_async_copy(o.at[:, cols(n)], o_hbm.at[0, :, cols(n)], o_sem.at[n])

    load_s = pltpu.make_async_copy(s_hbm.at[0], s, s_sem.at[0])
    load_s.start()
    for n in range(chunks):
        load_b(n).start()

    def wrap(index):
        return lax.rem(index + count, count)

    sibling = (k + 1, r)
    sibling_across = (k + 1, 1 - r)
    across = (k, 1 - r)
    next_one = (wrap(k + 1), r)
    next_two = (wrap(k + 3), r)

    barrier = pltpu.get_barrier_semaphore()

    def greet(*devices):
        for device in devices:
            pl.semaphore_signal(barrier, inc=1, device_id=device, device_id_type=MESH)

    @pl.when(even)
    def _():
        greet((wrap(k - 1), r), (wrap(k - 3), r), across)
        pl.semaphore_wait(barrier, 3)

    @pl.when(jnp.logical_not(even))
    def _():
        greet((k - 1, r), (k - 1, 1 - r))
        pl.semaphore_wait(barrier, 2)

    def remote(src, dst, kind, n, arrived, device):
        return pltpu.make_async_remote_copy(
            src_ref=src, dst_ref=dst, send_sem=send.at[kind, n], recv_sem=arrived.at[n],
            device_id=device, device_id_type=MESH,
        )

    def p_sibling(n):
        return remote(p.at[:, cols(n)], m1.at[own, cols(n)], 0, n, r1o, sibling)

    def p_across(n):
        return remote(p.at[:, cols(n)], m1.at[own, cols(n)], 1, n, r1c, sibling_across)

    def m1_own_sibling(n):
        return remote(m1.at[own, cols(n)], m2.at[own, cols(n)], 2, n, r2o, sibling)

    def m1_own_across(n):
        return remote(m1.at[own, cols(n)], m1.at[own, cols(n)], 3, n, r1c, across)

    def m1_cross_sibling(n):
        return remote(m1.at[cross, cols(n)], m2.at[cross, cols(n)], 4, n, r2c, sibling)

    def m2_own_across(n):
        return remote(m2.at[own, cols(n)], m2.at[own, cols(n)], 5, n, r2c, across)

    def p_next_two(n):
        return remote(p.at[:, cols(n)], m2.at[own, cols(n)], 0, n, r2o, next_two)

    def x_next_one(n):
        return remote(x.at[:, cols(n)], m1.at[own, cols(n)], 1, n, r1o, next_one)

    def landed(ref, part, n, arrived):
        remote(ref.at[part, cols(n)], ref.at[part, cols(n)], 0, n, arrived, across).wait_recv()

    def multiply(dst, left, right, n, scale):
        @pl.loop(0, rows // TILE)
        def _(t):
            at = pl.ds(pl.multiple_of(t * TILE, TILE), TILE)
            got = jnp.dot(left[at, :], right[:, cols(n)], preferred_element_type=jnp.float32)
            dst[at, cols(n)] = (got * scale).astype(jnp.bfloat16)

    def gain(j, at):
        row = table[pl.ds(phase[0, j], 1), at]
        return jnp.exp(0.1 * steps[0, j].astype(jnp.float32) * row)

    load_s.wait()
    gain_left = gain(1, slice(None))

    @pl.loop(0, rows // 64)
    def _(t):
        at = pl.ds(pl.multiple_of(t * 64, 64), 64)
        s[at, :] = (s[at, :].astype(jnp.float32) * gain_left).astype(jnp.bfloat16)

    @pl.loop(0, chunks)
    def _(n):
        load_b(n).wait()
        multiply(p, s, b, n, gain(0, cols(n)) * norm)

        @pl.when(even)
        def _():
            p_across(n).start()
            p_sibling(n).start()

        @pl.when(jnp.logical_not(even))
        def _():
            p_next_two(n).start()

    half = chunks // 2

    @pl.when(even)
    def _():
        def pass_m2(n):
            landed(m2, own, n, r2o)
            m2_own_across(n).start()

        @pl.loop(0, chunks + LAG)
        def _(n):
            @pl.when(n < chunks)
            def _():
                landed(m1, own, n, r1o)
                m1_own_across(n).start()
                m1_own_sibling(n).start()

            @pl.when(jnp.logical_and(lax.rem(n, 2) == 1, n < chunks))
            def _():
                pass_m2(n // 2)

            @pl.when(n >= LAG)
            def _():
                landed(m1, cross, n - LAG, r1c)
                m1_cross_sibling(n - LAG).start()
                multiply(x, p, m1, n - LAG, norm)

            @pl.when(n >= chunks)
            def _():
                pass_m2(half + n - chunks)

        @pl.loop(half + LAG, chunks)
        def _(n):
            pass_m2(n)

        @pl.loop(0, chunks)
        def _(n):
            landed(m2, cross, n, r2c)
            multiply(o, x, m2, n, norm)
            store_o(n).start()

        @pl.loop(0, chunks)
        def _(n):
            for copy in (p_sibling, p_across, m1_own_sibling, m1_own_across, m1_cross_sibling, m2_own_across):
                copy(n).wait_send()
            store_o(n).wait()

    @pl.when(jnp.logical_not(even))
    def _():
        @pl.loop(0, chunks)
        def _(n):
            landed(m1, own, n, r1o)
            landed(m1, cross, n, r1c)
            multiply(x, p, m1, n, norm)
            x_next_one(n).start()

        @pl.loop(0, chunks)
        def _(n):
            landed(m2, own, n, r2o)
            landed(m2, cross, n, r2c)
            multiply(o, x, m2, n, norm)
            store_o(n).start()

        @pl.loop(0, chunks)
        def _(n):
            for copy in (p_next_two, x_next_one):
                copy(n).wait_send()
            store_o(n).wait()


def shards(count, slice_ops, base_op, load_table, phase_idx, step_counts):
    _, rows, size = slice_ops.shape
    chunks = size // WIDTH
    bf16 = jnp.bfloat16
    dma = pltpu.SemaphoreType.DMA
    return pl.pallas_call(
        functools.partial(kernel, count),
        out_shape=jax.ShapeDtypeStruct(slice_ops.shape, bf16),
        in_specs=[
            pl.BlockSpec(memory_space=pl.ANY),
            pl.BlockSpec(memory_space=pl.ANY),
            pl.BlockSpec(memory_space=pltpu.VMEM),
            pl.BlockSpec(memory_space=pltpu.SMEM),
            pl.BlockSpec(memory_space=pltpu.SMEM),
        ],
        out_specs=pl.BlockSpec(memory_space=pl.ANY),
        scratch_shapes=[
            pltpu.VMEM((rows, size), bf16),
            pltpu.VMEM((size, size), bf16),
            pltpu.VMEM((rows, size), bf16),
            pltpu.VMEM((rows, size), bf16),
            pltpu.VMEM((size, size), bf16),
            pltpu.VMEM((size, size), bf16),
            pltpu.VMEM((rows, size), bf16),
            dma((1,)),
            dma((chunks,)),
            dma((chunks,)),
            dma((6, chunks)),
            dma((chunks,)),
            dma((chunks,)),
            dma((chunks,)),
            dma((chunks,)),
        ],
        compiler_params=pltpu.CompilerParams(
            collective_id=0, has_side_effects=True, vmem_limit_bytes=56 * 2**20
        ),
        cost_estimate=pl.CostEstimate(
            flops=6 * rows * size * size, bytes_accessed=2 * 4 * rows * size, transcendentals=0
        ),
    )(slice_ops, base_op, load_table, phase_idx, step_counts)


def solution(mesh):
    return jax.shard_map(
        functools.partial(shards, mesh.shape["tm"]),
        mesh=mesh,
        in_specs=(P("tm", "row", None), P(), P(), P("tm", None), P("tm", None)),
        out_specs=P("tm", "row", None),
        check_vma=False,
    )
```

```python
import functools
import math

import jax
import jax.numpy as jnp
from jax import lax
from jax.experimental import pallas as pl
from jax.experimental.pallas import tpu as pltpu
from jax.sharding import PartitionSpec as P

MESH = pl.DeviceIdType.MESH
WIDTH = 256
TILE = 512
SHARE = 1, 4


def kernel(
    count, s_hbm, b_hbm, table, phase, steps, o_hbm,
    s, b, p, x, m1, m2, o, q, y, s_sem, b_sem, o_sem, send, r1o, r1c, r2o, r2c, r1d, r2d, rq,
):
    rows, size = s.shape
    chunks = size // WIDTH
    norm = 1.0 / math.sqrt(size)
    k = lax.axis_index("tm")
    r = lax.axis_index("row")
    odd = lax.rem(k, 2)
    even = odd == 0
    own = pl.ds(pl.multiple_of(r * rows, rows), rows)
    cross = pl.ds(pl.multiple_of((1 - r) * rows, rows), rows)
    shared = q.shape[0]
    rest = rows - shared
    own_rest = pl.ds(pl.multiple_of(r * rows + shared, 128), rest)
    cross_rest = pl.ds(pl.multiple_of((1 - r) * rows + shared, 128), rest)
    cross_shared = pl.ds(pl.multiple_of((1 - r) * rows, rows), shared)

    def cols(n):
        return pl.ds(pl.multiple_of(n * WIDTH, WIDTH), WIDTH)

    def load_b(n):
        return pltpu.make_async_copy(b_hbm.at[:, cols(n)], b.at[:, cols(n)], b_sem.at[n])

    def store_o(n):
        return pltpu.make_async_copy(o.at[:, cols(n)], o_hbm.at[0, :, cols(n)], o_sem.at[n])

    load_s = pltpu.make_async_copy(s_hbm.at[0], s, s_sem.at[0])
    load_s.start()
    for n in range(chunks):
        load_b(n).start()

    def wrap(index):
        return lax.rem(index + count, count)

    sibling = (k + 1, r)
    sibling_across = (k + 1, 1 - r)
    across = (k, 1 - r)
    next_one = (wrap(k + 1), r)
    next_two = (wrap(k + 3), r)

    barrier = pltpu.get_barrier_semaphore()

    def greet(*devices):
        for device in devices:
            pl.semaphore_signal(barrier, inc=1, device_id=device, device_id_type=MESH)

    @pl.when(even)
    def _():
        greet((wrap(k - 1), r), (wrap(k - 3), r), across)
        pl.semaphore_wait(barrier, 3)

    @pl.when(jnp.logical_not(even))
    def _():
        greet((k - 1, r), (k - 1, 1 - r), across)
        pl.semaphore_wait(barrier, 3)

    def remote(src, dst, kind, n, arrived, device):
        return pltpu.make_async_remote_copy(
            src_ref=src, dst_ref=dst, send_sem=send.at[kind, n], recv_sem=arrived.at[n],
            device_id=device, device_id_type=MESH,
        )

    def p_sibling(n):
        return remote(p.at[:, cols(n)], m1.at[own, cols(n)], 0, n, r1o, sibling)

    def p_across(n):
        return remote(p.at[:, cols(n)], m1.at[own, cols(n)], 1, n, r1c, sibling_across)

    def m1_own_sibling(n):
        return remote(m1.at[own, cols(n)], m2.at[own, cols(n)], 2, n, r2o, sibling)

    def m1_own_across(n):
        return remote(m1.at[own_rest, cols(n)], m1.at[own_rest, cols(n)], 3, n, r1c, across)

    def m1_cross_sibling(n):
        return remote(m1.at[cross, cols(n)], m2.at[cross, cols(n)], 4, n, r2c, sibling)

    def m2_own_across(n):
        return remote(m2.at[own_rest, cols(n)], m2.at[own_rest, cols(n)], 5, n, r2c, across)

    def p_next_two(n):
        return remote(p.at[:, cols(n)], m2.at[own, cols(n)], 0, n, r2o, next_two)

    def x_next_one(n):
        return remote(x.at[:, cols(n)], m1.at[own, cols(n)], 1, n, r1o, next_one)

    def p_across_odd(n):
        return remote(p.at[pl.ds(0, shared), cols(n)], q.at[:, cols(n)], 2, n, rq, across)

    def q_next_two(n):
        return remote(q.at[:, cols(n)], m2.at[cross_shared, cols(n)], 3, n, r2d, next_two)

    def y_next_one(n):
        return remote(y.at[:, cols(n)], m1.at[cross_shared, cols(n)], 4, n, r1d, next_one)

    def landed(ref, part, n, arrived):
        remote(ref.at[part, cols(n)], ref.at[part, cols(n)], 0, n, arrived, across).wait_recv()

    def multiply(dst, left, right, n, scale, tile=TILE):
        @pl.loop(0, left.shape[0] // tile)
        def _(t):
            at = pl.ds(pl.multiple_of(t * tile, tile), tile)
            got = jnp.dot(left[at, :], right[:, cols(n)], preferred_element_type=jnp.float32)
            dst[at, cols(n)] = (got * scale).astype(jnp.bfloat16)

    def gain(j, at):
        row = table[pl.ds(phase[0, j], 1), at]
        return jnp.exp(0.1 * steps[0, j].astype(jnp.float32) * row)

    load_s.wait()
    gain_left = gain(1, slice(None))

    @pl.loop(0, rows // 64)
    def _(t):
        at = pl.ds(pl.multiple_of(t * 64, 64), 64)
        s[at, :] = (s[at, :].astype(jnp.float32) * gain_left).astype(jnp.bfloat16)

    @pl.loop(0, chunks)
    def _(n):
        load_b(n).wait()
        multiply(p, s, b, n, gain(0, cols(n)) * norm)

        @pl.when(even)
        def _():
            p_across(n).start()
            p_sibling(n).start()

        @pl.when(jnp.logical_not(even))
        def _():
            p_across_odd(n).start()
            p_next_two(n).start()

    half = chunks // 2

    @pl.when(even)
    def _():
        def pass_m2(n):
            landed(m2, own, n, r2o)
            m2_own_across(n).start()

        @pl.loop(0, chunks)
        def _(n):
            landed(m1, own, n, r1o)
            m1_own_across(n).start()
            m1_own_sibling(n).start()

            @pl.when(lax.rem(n, 2) == 1)
            def _():
                pass_m2(n // 2)

        @pl.loop(half, chunks)
        def _(n):
            pass_m2(n)

        @pl.loop(0, chunks)
        def _(n):
            landed(m1, cross_rest, n, r1c)
            landed(m1, cross_shared, n, r1d)
            m1_cross_sibling(n).start()
            multiply(x, p, m1, n, norm)

        @pl.loop(0, chunks)
        def _(n):
            landed(m2, cross_shared, n, r2d)
            landed(m2, cross_rest, n, r2c)
            multiply(o, x, m2, n, norm)
            store_o(n).start()

        @pl.loop(0, chunks)
        def _(n):
            for copy in (p_sibling, p_across, m1_own_sibling, m1_own_across, m1_cross_sibling, m2_own_across):
                copy(n).wait_send()
            store_o(n).wait()

    @pl.when(jnp.logical_not(even))
    def _():
        @pl.loop(0, chunks)
        def _(n):
            landed(m1, own, n, r1o)
            landed(m1, cross, n, r1c)
            multiply(x, p, m1, n, norm)
            x_next_one(n).start()
            landed(q, slice(None), n, rq)
            q_next_two(n).start()

        @pl.loop(0, chunks)
        def _(n):
            multiply(y, q, m1, n, norm, shared)
            y_next_one(n).start()

        @pl.loop(0, chunks)
        def _(n):
            landed(m2, own, n, r2o)
            landed(m2, cross, n, r2c)
            multiply(o, x, m2, n, norm)
            store_o(n).start()

        @pl.loop(0, chunks)
        def _(n):
            for copy in (p_next_two, x_next_one, p_across_odd, q_next_two, y_next_one):
                copy(n).wait_send()
            store_o(n).wait()


def shards(count, slice_ops, base_op, load_table, phase_idx, step_counts):
    _, rows, size = slice_ops.shape
    chunks = size // WIDTH
    shared = rows * SHARE[0] // SHARE[1]
    bf16 = jnp.bfloat16
    dma = pltpu.SemaphoreType.DMA
    return pl.pallas_call(
        functools.partial(kernel, count),
        out_shape=jax.ShapeDtypeStruct(slice_ops.shape, bf16),
        in_specs=[
            pl.BlockSpec(memory_space=pl.ANY),
            pl.BlockSpec(memory_space=pl.ANY),
            pl.BlockSpec(memory_space=pltpu.VMEM),
            pl.BlockSpec(memory_space=pltpu.SMEM),
            pl.BlockSpec(memory_space=pltpu.SMEM),
        ],
        out_specs=pl.BlockSpec(memory_space=pl.ANY),
        scratch_shapes=[
            pltpu.VMEM((rows, size), bf16),
            pltpu.VMEM((size, size), bf16),
            pltpu.VMEM((rows, size), bf16),
            pltpu.VMEM((rows, size), bf16),
            pltpu.VMEM((size, size), bf16),
            pltpu.VMEM((size, size), bf16),
            pltpu.VMEM((rows, size), bf16),
            pltpu.VMEM((shared, size), bf16),
            pltpu.VMEM((shared, size), bf16),
            dma((1,)),
            dma((chunks,)),
            dma((chunks,)),
            dma((6, chunks)),
            dma((chunks,)),
            dma((chunks,)),
            dma((chunks,)),
            dma((chunks,)),
            dma((chunks,)),
            dma((chunks,)),
            dma((chunks,)),
        ],
        compiler_params=pltpu.CompilerParams(
            collective_id=0, has_side_effects=True, vmem_limit_bytes=56 * 2**20
        ),
        cost_estimate=pl.CostEstimate(
            flops=6 * rows * size * size, bytes_accessed=2 * 4 * rows * size, transcendentals=0
        ),
    )(slice_ops, base_op, load_table, phase_idx, step_counts)


def solution(mesh):
    return jax.shard_map(
        functools.partial(shards, mesh.shape["tm"]),
        mesh=mesh,
        in_specs=(P("tm", "row", None), P(), P(), P("tm", None), P("tm", None)),
        out_specs=P("tm", "row", None),
        check_vma=False,
    )
```

```python
import functools
import math

import jax
import jax.numpy as jnp
from jax import lax
from jax.experimental import pallas as pl
from jax.experimental.pallas import tpu as pltpu
from jax.sharding import PartitionSpec as P

MESH = pl.DeviceIdType.MESH
WIDTH = 256
TILE = 512
SHARE = 1, 4


def kernel(
    count, s_hbm, b_hbm, table, phase, steps, o_hbm,
    s, b, p, x, m1, m2, o, q, y, s_sem, b_sem, o_sem, send, r1o, r1c, r2o, r2c, r1d, r2d, rq,
):
    rows, size = s.shape
    chunks = size // WIDTH
    norm = 1.0 / math.sqrt(size)
    k = lax.axis_index("tm")
    r = lax.axis_index("row")
    odd = lax.rem(k, 2)
    even = odd == 0
    own = pl.ds(pl.multiple_of(r * rows, rows), rows)
    cross = pl.ds(pl.multiple_of((1 - r) * rows, rows), rows)
    shared = q.shape[0]
    rest = rows - shared
    own_rest = pl.ds(pl.multiple_of(r * rows + shared, 128), rest)
    cross_rest = pl.ds(pl.multiple_of((1 - r) * rows + shared, 128), rest)
    cross_shared = pl.ds(pl.multiple_of((1 - r) * rows, rows), shared)

    def cols(n):
        return pl.ds(pl.multiple_of(n * WIDTH, WIDTH), WIDTH)

    def load_b(n):
        return pltpu.make_async_copy(b_hbm.at[:, cols(n)], b.at[:, cols(n)], b_sem.at[n])

    def store_o(n):
        return pltpu.make_async_copy(o.at[:, cols(n)], o_hbm.at[0, :, cols(n)], o_sem.at[n])

    load_s = pltpu.make_async_copy(s_hbm.at[0], s, s_sem.at[0])
    load_s.start()
    for n in range(chunks):
        load_b(n).start()

    def wrap(index):
        return lax.rem(index + count, count)

    sibling = (k + 1, r)
    sibling_across = (k + 1, 1 - r)
    across = (k, 1 - r)
    next_one = (wrap(k + 1), r)
    next_two = (wrap(k + 3), r)

    barrier = pltpu.get_barrier_semaphore()

    def greet(*devices):
        for device in devices:
            pl.semaphore_signal(barrier, inc=1, device_id=device, device_id_type=MESH)

    @pl.when(even)
    def _():
        greet((wrap(k - 1), r), (wrap(k - 3), r), across)
        pl.semaphore_wait(barrier, 3)

    @pl.when(jnp.logical_not(even))
    def _():
        greet((k - 1, r), (k - 1, 1 - r), across)
        pl.semaphore_wait(barrier, 3)

    def remote(src, dst, kind, n, arrived, device):
        return pltpu.make_async_remote_copy(
            src_ref=src, dst_ref=dst, send_sem=send.at[kind, n], recv_sem=arrived.at[n],
            device_id=device, device_id_type=MESH,
        )

    def p_sibling(n):
        return remote(p.at[:, cols(n)], m1.at[own, cols(n)], 0, n, r1o, sibling)

    def p_across(n):
        return remote(p.at[:, cols(n)], m1.at[own, cols(n)], 1, n, r1c, sibling_across)

    def m1_own_sibling(n):
        return remote(m1.at[own, cols(n)], m2.at[own, cols(n)], 2, n, r2o, sibling)

    def m1_own_across(n):
        return remote(m1.at[own_rest, cols(n)], m1.at[own_rest, cols(n)], 3, n, r1c, across)

    def m1_cross_sibling(n):
        return remote(m1.at[cross, cols(n)], m2.at[cross, cols(n)], 4, n, r2c, sibling)

    def m2_own_across(n):
        return remote(m2.at[own_rest, cols(n)], m2.at[own_rest, cols(n)], 5, n, r2c, across)

    def p_next_two(n):
        return remote(p.at[:, cols(n)], m2.at[own, cols(n)], 0, n, r2o, next_two)

    def x_next_one(n):
        return remote(x.at[:, cols(n)], m1.at[own, cols(n)], 1, n, r1o, next_one)

    def p_across_odd(n):
        return remote(p.at[pl.ds(0, shared), cols(n)], q.at[:, cols(n)], 2, n, rq, across)

    def q_next_two(n):
        return remote(q.at[:, cols(n)], m2.at[cross_shared, cols(n)], 3, n, r2d, next_two)

    def y_next_one(n):
        return remote(y.at[:, cols(n)], m1.at[cross_shared, cols(n)], 4, n, r1d, next_one)

    def landed(ref, part, n, arrived):
        remote(ref.at[part, cols(n)], ref.at[part, cols(n)], 0, n, arrived, across).wait_recv()

    def multiply(dst, left, right, n, scale, tile=TILE):
        @pl.loop(0, left.shape[0] // tile)
        def _(t):
            at = pl.ds(pl.multiple_of(t * tile, tile), tile)
            got = jnp.dot(left[at, :], right[:, cols(n)], preferred_element_type=jnp.float32)
            dst[at, cols(n)] = (got * scale).astype(jnp.bfloat16)

    def gain(j, at):
        row = table[pl.ds(phase[0, j], 1), at]
        return jnp.exp(0.1 * steps[0, j].astype(jnp.float32) * row)

    load_s.wait()
    gain_left = gain(1, slice(None))

    @pl.loop(0, rows // 64)
    def _(t):
        at = pl.ds(pl.multiple_of(t * 64, 64), 64)
        s[at, :] = (s[at, :].astype(jnp.float32) * gain_left).astype(jnp.bfloat16)

    @pl.loop(0, chunks)
    def _(n):
        load_b(n).wait()
        multiply(p, s, b, n, gain(0, cols(n)) * norm)

        @pl.when(even)
        def _():
            p_across(n).start()
            p_sibling(n).start()

        @pl.when(jnp.logical_not(even))
        def _():
            p_across_odd(n).start()
            p_next_two(n).start()

    half = chunks // 2

    @pl.when(even)
    def _():
        def pass_m2(n):
            landed(m2, own, n, r2o)
            m2_own_across(n).start()

        @pl.loop(0, chunks)
        def _(n):
            landed(m1, own, n, r1o)
            m1_own_across(n).start()
            m1_own_sibling(n).start()

            @pl.when(lax.rem(n, 2) == 1)
            def _():
                pass_m2(n // 2)

        @pl.loop(half, chunks)
        def _(n):
            pass_m2(n)

        @pl.loop(0, chunks)
        def _(n):
            landed(m1, cross_rest, n, r1c)
            landed(m1, cross_shared, n, r1d)
            m1_cross_sibling(n).start()
            multiply(x, p, m1, n, norm)

        @pl.loop(0, chunks)
        def _(n):
            landed(m2, cross_shared, n, r2d)
            landed(m2, cross_rest, n, r2c)
            multiply(o, x, m2, n, norm)
            store_o(n).start()

        @pl.loop(0, chunks)
        def _(n):
            for copy in (p_sibling, p_across, m1_own_sibling, m1_own_across, m1_cross_sibling, m2_own_across):
                copy(n).wait_send()
            store_o(n).wait()

    @pl.when(jnp.logical_not(even))
    def _():
        @pl.loop(0, chunks)
        def _(n):
            landed(m1, own, n, r1o)
            landed(m1, cross, n, r1c)
            multiply(x, p, m1, n, norm)
            x_next_one(n).start()

        @pl.loop(0, chunks)
        def _(n):
            landed(q, slice(None), n, rq)

        @pl.loop(0, chunks)
        def _(n):
            multiply(y, q, m1, n, norm, shared)
            y_next_one(n).start()
            q_next_two(n).start()

        @pl.loop(0, chunks)
        def _(n):
            landed(m2, own, n, r2o)
            landed(m2, cross, n, r2c)
            multiply(o, x, m2, n, norm)
            store_o(n).start()

        @pl.loop(0, chunks)
        def _(n):
            for copy in (p_next_two, x_next_one, p_across_odd, q_next_two, y_next_one):
                copy(n).wait_send()
            store_o(n).wait()


def shards(count, slice_ops, base_op, load_table, phase_idx, step_counts):
    _, rows, size = slice_ops.shape
    chunks = size // WIDTH
    shared = rows * SHARE[0] // SHARE[1]
    bf16 = jnp.bfloat16
    dma = pltpu.SemaphoreType.DMA
    return pl.pallas_call(
        functools.partial(kernel, count),
        out_shape=jax.ShapeDtypeStruct(slice_ops.shape, bf16),
        in_specs=[
            pl.BlockSpec(memory_space=pl.ANY),
            pl.BlockSpec(memory_space=pl.ANY),
            pl.BlockSpec(memory_space=pltpu.VMEM),
            pl.BlockSpec(memory_space=pltpu.SMEM),
            pl.BlockSpec(memory_space=pltpu.SMEM),
        ],
        out_specs=pl.BlockSpec(memory_space=pl.ANY),
        scratch_shapes=[
            pltpu.VMEM((rows, size), bf16),
            pltpu.VMEM((size, size), bf16),
            pltpu.VMEM((rows, size), bf16),
            pltpu.VMEM((rows, size), bf16),
            pltpu.VMEM((size, size), bf16),
            pltpu.VMEM((size, size), bf16),
            pltpu.VMEM((rows, size), bf16),
            pltpu.VMEM((shared, size), bf16),
            pltpu.VMEM((shared, size), bf16),
            dma((1,)),
            dma((chunks,)),
            dma((chunks,)),
            dma((6, chunks)),
            dma((chunks,)),
            dma((chunks,)),
            dma((chunks,)),
            dma((chunks,)),
            dma((chunks,)),
            dma((chunks,)),
            dma((chunks,)),
        ],
        compiler_params=pltpu.CompilerParams(
            collective_id=0, has_side_effects=True, vmem_limit_bytes=56 * 2**20
        ),
        cost_estimate=pl.CostEstimate(
            flops=6 * rows * size * size, bytes_accessed=2 * 4 * rows * size, transcendentals=0
        ),
    )(slice_ops, base_op, load_table, phase_idx, step_counts)


def solution(mesh):
    return jax.shard_map(
        functools.partial(shards, mesh.shape["tm"]),
        mesh=mesh,
        in_specs=(P("tm", "row", None), P(), P(), P("tm", None), P("tm", None)),
        out_specs=P("tm", "row", None),
        check_vma=False,
    )
```

```python
import functools
import math

import jax
import jax.numpy as jnp
from jax import lax
from jax.experimental import pallas as pl
from jax.experimental.pallas import tpu as pltpu
from jax.sharding import PartitionSpec as P

MESH = pl.DeviceIdType.MESH
WIDTH = 256
TILE = 512
SHARE = 1, 4


def kernel(
    count, s_hbm, b_hbm, table, phase, steps, o_hbm,
    s, b, p, x, m1, m2, o, q, y, s_sem, b_sem, o_sem, send, r1o, r1c, r2o, r2c, r1d, r2d, rq,
):
    rows, size = s.shape
    chunks = size // WIDTH
    norm = 1.0 / math.sqrt(size)
    k = lax.axis_index("tm")
    r = lax.axis_index("row")
    odd = lax.rem(k, 2)
    even = odd == 0
    own = pl.ds(pl.multiple_of(r * rows, rows), rows)
    cross = pl.ds(pl.multiple_of((1 - r) * rows, rows), rows)
    shared = q.shape[0]
    rest = rows - shared
    own_rest = pl.ds(pl.multiple_of(r * rows + shared, 128), rest)
    cross_rest = pl.ds(pl.multiple_of((1 - r) * rows + shared, 128), rest)
    cross_shared = pl.ds(pl.multiple_of((1 - r) * rows, rows), shared)

    def cols(n):
        return pl.ds(pl.multiple_of(n * WIDTH, WIDTH), WIDTH)

    def load_b(n):
        return pltpu.make_async_copy(b_hbm.at[:, cols(n)], b.at[:, cols(n)], b_sem.at[n])

    def store_o(n):
        return pltpu.make_async_copy(o.at[:, cols(n)], o_hbm.at[0, :, cols(n)], o_sem.at[n])

    quarter = rows // 4

    def load_s(n):
        at = pl.ds(pl.multiple_of(n * quarter, quarter), quarter)
        return pltpu.make_async_copy(s_hbm.at[0, at], s.at[at], s_sem.at[n])

    for n in range(4):
        load_s(n).start()
    for n in range(chunks):
        load_b(n).start()

    def wrap(index):
        return lax.rem(index + count, count)

    sibling = (k + 1, r)
    sibling_across = (k + 1, 1 - r)
    across = (k, 1 - r)
    next_one = (wrap(k + 1), r)
    next_two = (wrap(k + 3), r)

    barrier = pltpu.get_barrier_semaphore()

    def greet(*devices):
        for device in devices:
            pl.semaphore_signal(barrier, inc=1, device_id=device, device_id_type=MESH)

    @pl.when(even)
    def _():
        greet((wrap(k - 1), r), (wrap(k - 3), r), across)
        pl.semaphore_wait(barrier, 3)

    @pl.when(jnp.logical_not(even))
    def _():
        greet((k - 1, r), (k - 1, 1 - r), across)
        pl.semaphore_wait(barrier, 3)

    def remote(src, dst, kind, n, arrived, device):
        return pltpu.make_async_remote_copy(
            src_ref=src, dst_ref=dst, send_sem=send.at[kind, n], recv_sem=arrived.at[n],
            device_id=device, device_id_type=MESH,
        )

    def p_sibling(n):
        return remote(p.at[:, cols(n)], m1.at[own, cols(n)], 0, n, r1o, sibling)

    def p_across(n):
        return remote(p.at[:, cols(n)], m1.at[own, cols(n)], 1, n, r1c, sibling_across)

    def m1_own_sibling(n):
        return remote(m1.at[own, cols(n)], m2.at[own, cols(n)], 2, n, r2o, sibling)

    def m1_own_across(n):
        return remote(m1.at[own_rest, cols(n)], m1.at[own_rest, cols(n)], 3, n, r1c, across)

    def m1_cross_sibling(n):
        return remote(m1.at[cross, cols(n)], m2.at[cross, cols(n)], 4, n, r2c, sibling)

    def m2_own_across(n):
        return remote(m2.at[own_rest, cols(n)], m2.at[own_rest, cols(n)], 5, n, r2c, across)

    def p_next_two(n):
        return remote(p.at[:, cols(n)], m2.at[own, cols(n)], 0, n, r2o, next_two)

    def x_next_one(n):
        return remote(x.at[:, cols(n)], m1.at[own, cols(n)], 1, n, r1o, next_one)

    def p_across_odd(n):
        return remote(p.at[pl.ds(0, shared), cols(n)], q.at[:, cols(n)], 2, n, rq, across)

    def q_next_two(n):
        return remote(q.at[:, cols(n)], m2.at[cross_shared, cols(n)], 3, n, r2d, next_two)

    def y_next_one(n):
        return remote(y.at[:, cols(n)], m1.at[cross_shared, cols(n)], 4, n, r1d, next_one)

    def landed(ref, part, n, arrived):
        remote(ref.at[part, cols(n)], ref.at[part, cols(n)], 0, n, arrived, across).wait_recv()

    def multiply(dst, left, right, n, scale, tile=TILE):
        @pl.loop(0, left.shape[0] // tile)
        def _(t):
            at = pl.ds(pl.multiple_of(t * tile, tile), tile)
            got = jnp.dot(left[at, :], right[:, cols(n)], preferred_element_type=jnp.float32)
            dst[at, cols(n)] = (got * scale).astype(jnp.bfloat16)

    def gain(j, at):
        row = table[pl.ds(phase[0, j], 1), at]
        return jnp.exp(0.1 * steps[0, j].astype(jnp.float32) * row)

    gain_left = gain(1, slice(None))

    @pl.loop(0, 4)
    def _(t):
        load_s(t).wait()
        at = pl.ds(pl.multiple_of(t * quarter, quarter), quarter)
        s[at, :] = (s[at, :].astype(jnp.float32) * gain_left).astype(jnp.bfloat16)

    @pl.loop(0, chunks)
    def _(n):
        load_b(n).wait()
        multiply(p, s, b, n, gain(0, cols(n)) * norm)

        @pl.when(even)
        def _():
            p_across(n).start()
            p_sibling(n).start()

        @pl.when(jnp.logical_not(even))
        def _():
            p_across_odd(n).start()
            p_next_two(n).start()

    half = chunks // 2

    @pl.when(even)
    def _():
        def pass_m2(n):
            landed(m2, own, n, r2o)
            m2_own_across(n).start()

        @pl.loop(0, chunks)
        def _(n):
            landed(m1, own, n, r1o)
            m1_own_across(n).start()
            m1_own_sibling(n).start()

            @pl.when(lax.rem(n, 2) == 1)
            def _():
                pass_m2(n // 2)

        @pl.loop(half, chunks)
        def _(n):
            pass_m2(n)

        @pl.loop(0, chunks)
        def _(n):
            landed(m1, cross_rest, n, r1c)
            landed(m1, cross_shared, n, r1d)
            m1_cross_sibling(n).start()
            multiply(x, p, m1, n, norm)

        @pl.loop(0, chunks)
        def _(n):
            landed(m2, cross_shared, n, r2d)
            landed(m2, cross_rest, n, r2c)
            multiply(o, x, m2, n, norm)
            store_o(n).start()

        @pl.loop(0, chunks)
        def _(n):
            for copy in (p_sibling, p_across, m1_own_sibling, m1_own_across, m1_cross_sibling, m2_own_across):
                copy(n).wait_send()
            store_o(n).wait()

    @pl.when(jnp.logical_not(even))
    def _():
        @pl.loop(0, chunks)
        def _(n):
            landed(m1, own, n, r1o)
            landed(m1, cross, n, r1c)
            multiply(x, p, m1, n, norm)
            x_next_one(n).start()

        @pl.loop(0, chunks)
        def _(n):
            landed(q, slice(None), n, rq)

        @pl.loop(0, chunks)
        def _(n):
            multiply(y, q, m1, n, norm, shared)
            y_next_one(n).start()
            q_next_two(n).start()

        @pl.loop(0, chunks)
        def _(n):
            landed(m2, own, n, r2o)
            landed(m2, cross, n, r2c)
            multiply(o, x, m2, n, norm)
            store_o(n).start()

        @pl.loop(0, chunks)
        def _(n):
            for copy in (p_next_two, x_next_one, p_across_odd, q_next_two, y_next_one):
                copy(n).wait_send()
            store_o(n).wait()


def shards(count, slice_ops, base_op, load_table, phase_idx, step_counts):
    _, rows, size = slice_ops.shape
    chunks = size // WIDTH
    shared = rows * SHARE[0] // SHARE[1]
    bf16 = jnp.bfloat16
    dma = pltpu.SemaphoreType.DMA
    return pl.pallas_call(
        functools.partial(kernel, count),
        out_shape=jax.ShapeDtypeStruct(slice_ops.shape, bf16),
        in_specs=[
            pl.BlockSpec(memory_space=pl.ANY),
            pl.BlockSpec(memory_space=pl.ANY),
            pl.BlockSpec(memory_space=pltpu.VMEM),
            pl.BlockSpec(memory_space=pltpu.SMEM),
            pl.BlockSpec(memory_space=pltpu.SMEM),
        ],
        out_specs=pl.BlockSpec(memory_space=pl.ANY),
        scratch_shapes=[
            pltpu.VMEM((rows, size), bf16),
            pltpu.VMEM((size, size), bf16),
            pltpu.VMEM((rows, size), bf16),
            pltpu.VMEM((rows, size), bf16),
            pltpu.VMEM((size, size), bf16),
            pltpu.VMEM((size, size), bf16),
            pltpu.VMEM((rows, size), bf16),
            pltpu.VMEM((shared, size), bf16),
            pltpu.VMEM((shared, size), bf16),
            dma((4,)),
            dma((chunks,)),
            dma((chunks,)),
            dma((6, chunks)),
            dma((chunks,)),
            dma((chunks,)),
            dma((chunks,)),
            dma((chunks,)),
            dma((chunks,)),
            dma((chunks,)),
            dma((chunks,)),
        ],
        compiler_params=pltpu.CompilerParams(
            collective_id=0, has_side_effects=True, vmem_limit_bytes=56 * 2**20
        ),
        cost_estimate=pl.CostEstimate(
            flops=6 * rows * size * size, bytes_accessed=2 * 4 * rows * size, transcendentals=0
        ),
    )(slice_ops, base_op, load_table, phase_idx, step_counts)


def solution(mesh):
    return jax.shard_map(
        functools.partial(shards, mesh.shape["tm"]),
        mesh=mesh,
        in_specs=(P("tm", "row", None), P(), P(), P("tm", None), P("tm", None)),
        out_specs=P("tm", "row", None),
        check_vma=False,
    )
```
